32 devices in a mesh: grp: 2 (over x), band: 16 (over z, y, core).
Axes of the slice: x: 2, y: 2, z: 4, core: 2. Of those that a mesh axis runs over, the one named last changes fastest.
Arguments:
- orbitals: float32 [6, 64, 128, 128], P('grp', 'band'), parts along dimension 0, may hold values from -6 to 6
- band_ids: int32 [6], P('grp'), parts along dimension 0, may hold values from 0 to 2, each once
- occupations: float32 [6], P('grp'), parts along dimension 0, may hold values from 0.1 to 1
- screen: float32 [64, 128, 128], P('band'), may hold values from 0.2 to 2
Outputs:
- exchange: float32 [6, 64, 128, 128], P('grp', 'band'), parts along dimension 0
- energy: float32 [2], P('grp'), parts along dimension 0
The draws below stay inside these ranges and needn't reach their ends.
There are 2 independent parts, one for each index of `grp`. The reference program is written for one: setup_inputs(seed, part) draws one part's arguments, and reference() takes and returns one part's arrays. A program takes and returns all parts, laid end to end along the dimension named above; an argument that names none is the same for every part. Nothing has to cross between parts.
Inputs may be any that keep to these rules, and one draw needn't show every extreme that they name: `band_ids`: each band number appears in exactly one slot.
All inputs are finite; a program needn't handle non-finite values.
Results may differ from the reference program's by a relative error of at most 0.00002.
Values sent between devices are 32-bit elements; how exact they have to be, the bound alone decides.
A program may use at most 64 MiB of HBM per device.

```python
import math
import jax
import jax.numpy as jnp
from jax import lax

NBANDS = 3
GY = 128
GZ = 128
SWEEPS = 4
GX = 64


def draw_orbitals(key, part):
    first = jax.random.fold_in(key, 0)
    position = jnp.arange(GX, dtype=jnp.float32) / max(GX - 1, 1)
    envelope = 0.7 + 0.6 * position
    base = jnp.clip(jax.random.normal(first, (NBANDS, GX, GY, GZ), jnp.float32), -4.0, 4.0)
    return (base * envelope[None, :, None, None]).astype(jnp.float32)


def block_scale(key, dims, shards, low, top_value):
    def one(axis_at, shards_of):
        steps = jax.random.uniform(jax.random.fold_in(jax.random.fold_in(key, 6), axis_at), (shards_of,), jnp.float32, low / len(shards), top_value / len(shards))
        return jnp.repeat(jnp.exp(steps), dims[axis_at] // shards_of).reshape((-1,) + (1,) * (len(dims) - axis_at - 1))

    factor_of = one(*shards[0])
    for cut in shards[1:]:
        factor_of = factor_of * one(*cut)
    return factor_of


def setup_inputs(seed: int = 0, part: int = 0) -> dict:
    splits = jax.random.split(jax.random.key(seed), 5)
    part_splits = jax.random.split(jax.random.fold_in(splits[4], part), 5)
    orbitals = draw_orbitals(jax.random.fold_in(jax.random.fold_in(splits[4], part), 71), part)
    band_ids = jax.random.permutation(part_splits[1], NBANDS).astype(jnp.int32)
    occupations = jnp.clip(jnp.exp(jax.random.uniform(part_splits[2], (NBANDS,), jnp.float32, math.log(0.1), math.log(1.0))), 0.1, 1.0)
    screen = jnp.clip(jnp.exp(math.log(2.0) - 2.3025851 * jax.random.uniform(splits[3], (GX, GY, GZ), jnp.float32) ** block_scale(splits[3], (GX, GY, GZ), ((0, 16),), -0.2, 0.2)), 0.2, 2.0)
    return dict(orbitals=orbitals, band_ids=band_ids, occupations=occupations, screen=screen)


def sweeps(rho, screen):
    diag = 6.0 + screen
    lead = ((0, 0),) * (rho.ndim - 3)
    phi = jnp.zeros_like(rho)
    for sweep in range(SWEEPS):
        padded = jnp.pad(phi, lead + ((1, 1), (1, 1), (1, 1)))
        near = padded[..., 2:, 1:-1, 1:-1] + padded[..., :-2, 1:-1, 1:-1]
        near = near + padded[..., 1:-1, 2:, 1:-1] + padded[..., 1:-1, :-2, 1:-1]
        near = near + padded[..., 1:-1, 1:-1, 2:] + padded[..., 1:-1, 1:-1, :-2]
        phi = phi + 0.8 * (rho - (diag * phi - near)) / diag
    return phi


def reference(orbitals, band_ids, occupations, screen):
    occ = occupations[band_ids]
    weighted = occ[:, None, None, None] * orbitals

    def one_band(single):
        phi = sweeps(single[None] * orbitals, screen)
        return -jnp.sum(weighted * phi, axis=0)

    exchange = lax.map(one_band, orbitals)
    cells = GX * GY * GZ
    energy = (0.5 / cells) * jnp.sum(weighted * exchange)
    return exchange, energy.reshape(1).astype(jnp.float32)
```

```python
import functools

import jax
import jax.numpy as jnp
from jax import lax
from jax.experimental import pallas as pl
from jax.experimental.pallas import tpu as pltpu
from jax.sharding import PartitionSpec as P

LO, HI = 0, 1
PAD = 8


def radices_of(count):
    out = []
    while count > 1:
        radix = 4 if count % 4 == 0 else (2 if count % 2 == 0 else count)
        out.append(radix)
        count //= radix
    return out


def kernel(
    dims, cells,
    psi_hbm, screen_hbm, ids_ref, occs_ref, exch_hbm, energy_ref,
    psi, scr, c, usend, urecv, f1, f2, f3, ex, eslots,
    local_sem, out_sem, send_sem, recv_sem, fsend_sem, frecv_sem, esend_sem, erecv_sem,
):
    ngrp, n, nb, planes, gy, gz = dims
    pairs = [(i, j) for i in range(nb) for j in range(i, nb)]
    me = lax.axis_index("band")
    grp = lax.axis_index("grp")
    has = (me > 0, me < n - 1)
    near = (me - 1, me + 1)
    radices = radices_of(n)

    load_psi = pltpu.make_async_copy(psi_hbm, psi.at[:, pl.ds(2, planes)], local_sem.at[0])
    load_scr = pltpu.make_async_copy(screen_hbm, scr, local_sem.at[1])
    load_scr.start()
    load_psi.start()

    def rounds():
        stride, base = 1, 0
        for number, radix in enumerate(radices):
            digit = (me // stride) % radix
            peers = []
            for k in range(1, radix):
                other = (digit + k) % radix
                peers.append((k, other, me + (other - digit) * stride))
            yield number, base, radix, digit, peers
            base += radix
            stride *= radix

    barrier = pltpu.get_barrier_semaphore()
    for side in (LO, HI):
        @pl.when(has[side])
        def _():
            pl.semaphore_signal(barrier, inc=1, device_id={"band": near[side]})
    others = 0
    if ngrp == 2:
        pl.semaphore_signal(barrier, inc=1, device_id={"grp": 1 - grp})
        others += 1
    for _, _, _, _, peers in rounds():
        for _, _, peer in peers:
            pl.semaphore_signal(barrier, inc=1, device_id={"band": peer})
            others += 1
    pl.semaphore_wait(barrier, others + has[LO].astype(jnp.int32) + has[HI].astype(jnp.int32))

    rows = gy // 2 if ngrp == 2 else gy
    mine = pl.ds(pl.multiple_of(grp * rows, 8), rows) if ngrp == 2 else pl.ds(0, gy)
    theirs = pl.ds(pl.multiple_of((1 - grp) * rows, 8), rows) if ngrp == 2 else pl.ds(0, gy)

    def halo(side, depth):
        return 2 - depth if side == LO else planes + 1 + depth

    def own(side, depth):
        return planes - depth if side == LO else depth - 1

    def copy(side, number):
        depth = number // 2 + 1
        if number == 4:
            src, dst = usend.at[side], urecv.at[side]
        elif number % 2 == 0:
            src = psi_hbm.at[:, pl.ds(own(side, depth), 1)]
            dst = psi.at[:, pl.ds(halo(side, depth), 1)]
        else:
            src = c.at[own(side, depth) + 2, mine]
            dst = c.at[halo(side, depth), mine]
        return pltpu.make_async_remote_copy(
            src_ref=src, dst_ref=dst,
            send_sem=send_sem.at[side, number], recv_sem=recv_sem.at[side, number],
            device_id={"band": near[1 - side]},
        )

    def send(number):
        for side in (LO, HI):
            @pl.when(has[1 - side])
            def _():
                copy(side, number).start()

    def arrived(number):
        for side in (LO, HI):
            @pl.when(has[side])
            def _():
                copy(side, number).wait_recv()

    def forward(side, depth, rows_at):
        where = c.at[halo(side, depth), rows_at]
        return pltpu.make_async_remote_copy(
            src_ref=where, dst_ref=where,
            send_sem=fsend_sem.at[side, depth - 1], recv_sem=frecv_sem.at[side, depth - 1],
            device_id={"grp": 1 - grp},
        )

    def screen_arrived(depth):
        arrived(2 * depth - 1)
        if ngrp == 2:
            for side in (LO, HI):
                @pl.when(has[side])
                def _():
                    forward(side, depth, mine).start()
            for side in (LO, HI):
                @pl.when(has[side])
                def _():
                    forward(side, depth, theirs).wait_recv()

    send(0)
    load_scr.wait()
    for p in (0, planes - 1):
        c[p + 2] = 0.8 / (6.0 + scr[p])
    send(1)
    send(2)
    for p in range(1, planes - 1):
        c[p + 2] = 0.8 / (6.0 + scr[p])
    send(3)
    load_psi.wait()
    for side in (LO, HI):
        p = own(side, 3) + 2
        root = jnp.sqrt(c[p])
        for b in range(nb):
            usend[side, b] = root * psi[b, p]
    send(4)

    for side in (LO, HI):
        @pl.when(jnp.logical_not(has[side]))
        def _():
            at = 0 if side == LO else planes + 2
            for d in range(2):
                c[at + d] = jnp.zeros((gy, gz), jnp.float32)
                for b in range(nb):
                    psi[b, at + d] = jnp.zeros((gy, gz), jnp.float32)
            for b in range(nb):
                urecv[side, b] = jnp.zeros((gy, gz), jnp.float32)

    occ = []
    for s in range(nb):
        total = jnp.float32(0.0)
        for b in range(nb):
            total = total + jnp.where(ids_ref[s] == b, occs_ref[b], jnp.float32(0.0))
        occ.append(total)

    zeros = jnp.zeros((PAD, gz), jnp.float32)
    for buf in (f1, f2, f3):
        count = buf.shape[1]

        def clear(at, carry, buf=buf, count=count):
            for k in range(len(pairs)):
                buf[k, at, pl.ds(0, PAD)] = zeros
                buf[k, at, pl.ds(PAD + gy, PAD)] = zeros
            return carry

        lax.fori_loop(0, count, clear, 0)

    lanes = lax.broadcasted_iota(jnp.int32, (gy, gz), 1)
    first, last = lanes == 0, lanes == gz - 1

    def pair_of(k):
        i = jnp.int32(0)
        start = jnp.int32(0)
        at = 0
        for b in range(1, nb):
            at += nb - b + 1
            over = (k >= at).astype(jnp.int32)
            i = i + over
            start = start + over * (nb - b + 1)
        return i, i + k - start

    def lateral(buf, k, at):
        mid = buf[k, at, pl.ds(PAD, gy)]
        total = buf[k, at, pl.ds(PAD - 1, gy)] + buf[k, at, pl.ds(PAD + 1, gy)]
        total = total + jnp.where(first, 0.0, pltpu.roll(mid, 1, 1))
        total = total + jnp.where(last, 0.0, pltpu.roll(mid, gz - 1, 1))
        return mid, total

    def plane_pair(lo, hi):
        def each(body):
            def outer(t, carry):
                body(lo + t * (hi - lo), t)
                return carry

            lax.fori_loop(0, 2, outer, 0)

        return each

    def pairwise(body):
        def step(k, carry):
            i, j = pair_of(k)
            body(k, i, j)
            return carry

        lax.fori_loop(0, len(pairs), step, 0)

    def start_sweep(lo, hi):
        def plane(p, t):
            def one(k, i, j):
                f1[k, p, pl.ds(PAD, gy)] = c[p] * (psi[i, p] * psi[j, p])

            pairwise(one)

        plane_pair(lo, hi)(plane)

    def second(lo, hi, outer=False):
        def plane(p, t):
            def one(k, i, j):
                mid, total = lateral(f1, k, p)
                if outer:
                    total = total + f1[k, p + 1 - 2 * t, pl.ds(PAD, gy)]
                else:
                    total = total + f1[k, p - 1, pl.ds(PAD, gy)] + f1[k, p + 1, pl.ds(PAD, gy)]
                f2[k, p, pl.ds(PAD, gy)] = 1.2 * mid + c[p] * total

            pairwise(one)

        plane_pair(lo, hi)(plane)

    def third(lo, hi):
        def plane(p, t):
            def one(k, i, j):
                mid, total = lateral(f2, k, p)
                total = total + f2[k, p - 1, pl.ds(PAD, gy)] + f2[k, p + 1, pl.ds(PAD, gy)]
                total = total + psi[i, p] * psi[j, p]
                f3[k, p - 1, pl.ds(PAD, gy)] = 0.2 * mid + c[p] * total

            pairwise(one)

        plane_pair(lo, hi)(plane)

    def fourth(lo, hi):
        def plane(p, t):
            done = set()
            for k, (i, j) in enumerate(pairs):
                mid, total = lateral(f3, k, p - 1)
                total = total + f3[k, p - 2, pl.ds(PAD, gy)] + f3[k, p, pl.ds(PAD, gy)]
                total = total + psi[i, p] * psi[j, p]
                phi = 0.2 * mid + c[p] * total
                for a, b in {(i, j), (j, i)}:
                    term = (occ[b] * psi[b, p]) * phi
                    ex[a, p - 2] = ex[a, p - 2] - term if a in done else -term
                    done.add(a)

        plane_pair(lo, hi)(plane)

    m = planes - 1 + 2
    start_sweep(2, m)
    start_sweep(3, m - 1)
    second(3, m - 1)
    arrived(0)
    screen_arrived(1)
    start_sweep(1, m + 1)
    second(2, m)
    third(3, m - 1)
    arrived(2)
    screen_arrived(2)
    start_sweep(0, m + 2)
    second(1, m + 1)
    third(2, m)

    def energy_plane(p, acc):
        def one(k, acc):
            i, j = pair_of(k)
            a, b, d = (buf[k, at, pl.ds(PAD, gy)] for buf, at in ((f1, p), (f2, p), (f3, p - 1)))
            weight = jnp.float32(0.0)
            for number, (x, y) in enumerate(pairs):
                weight = jnp.where(k == number, (1.0 if x == y else 2.0) * occ[x] * occ[y], weight)
            value = psi[i, p] * psi[j, p] * b + (b - a) * (d - a) * (1.25 * (6.0 + scr[p - 2]))
            return acc + weight * jnp.sum(value.reshape(gy // 8, 8, gz), axis=0)

        return lax.fori_loop(0, len(pairs), one, acc)

    local = lax.fori_loop(2, planes + 2, energy_plane, jnp.zeros((8, gz), jnp.float32))

    def ecopy(number, base, digit, k, slot, peer):
        return pltpu.make_async_remote_copy(
            src_ref=eslots.at[base + digit], dst_ref=eslots.at[base + slot],
            send_sem=esend_sem.at[base + k], recv_sem=erecv_sem.at[base + slot],
            device_id={"band": peer},
        )

    def esend(entry, value):
        number, base, radix, digit, peers = entry
        eslots[base + digit] = value
        for k, other, peer in peers:
            ecopy(number, base, digit, k, digit, peer).start()

    def ewait(entry):
        number, base, radix, digit, peers = entry
        for k, other, peer in peers:
            ecopy(number, base, digit, k, other, peer).wait_recv()
        total = eslots[base]
        for r in range(1, radix):
            total = total + eslots[base + r]
        return total

    schedule = list(rounds())
    if schedule:
        esend(schedule[0], local)

    second(0, m + 2, outer=True)
    third(1, m + 1)
    fourth(3, m - 1)

    def out_copy(p, slot):
        return pltpu.make_async_copy(
            ex.at[:, pl.ds(p, 1)], exch_hbm.at[:, pl.ds(p, 1)], out_sem.at[slot]
        )

    for p in range(1, planes - 1):
        out_copy(p, p).start()
    fourth(2, m)

    for at, entry in enumerate(schedule):
        local = ewait(entry)
        if at + 1 < len(schedule):
            esend(schedule[at + 1], local)
    energy_ref[0] = (-0.5 / cells) * jnp.sum(local)

    arrived(4)
    for side in (LO, HI):
        p = 2 if side == LO else m
        step = -1 if side == LO else 1
        factor = c[p] * c[p + step] * c[p + 2 * step]
        total = sum((occ[b] * psi[b, p]) * urecv[side, b] for b in range(nb))
        total = total * factor
        for b in range(nb):
            ex[b, p - 2] = ex[b, p - 2] - total * urecv[side, b]
    for p in (0, planes - 1):
        out_copy(p, p).start()

    for number in range(5):
        for side in (LO, HI):
            @pl.when(has[1 - side])
            def _():
                copy(side, number).wait_send()
    if ngrp == 2:
        for depth in (1, 2):
            for side in (LO, HI):
                @pl.when(has[side])
                def _():
                    forward(side, depth, mine).wait_send()
    for number, base, radix, digit, peers in schedule:
        for k, other, peer in peers:
            ecopy(number, base, digit, k, digit, peer).wait_send()
    for p in range(planes):
        out_copy(p, p).wait()


def body(orbitals, band_ids, occupations, screen):
    nb, planes, gy, gz = orbitals.shape
    ngrp, n = lax.axis_size("grp"), lax.axis_size("band")
    npairs = nb * (nb + 1) // 2
    slots = sum(radices_of(n)) + 1
    f32 = jnp.float32
    dma = pltpu.SemaphoreType.DMA
    exchange, energy = pl.pallas_call(
        functools.partial(kernel, (ngrp, n, nb, planes, gy, gz), float(planes * n * gy * gz)),
        out_shape=(
            jax.ShapeDtypeStruct((nb, planes, gy, gz), f32),
            jax.ShapeDtypeStruct((1,), f32),
        ),
        in_specs=[
            pl.BlockSpec(memory_space=pl.ANY),
            pl.BlockSpec(memory_space=pl.ANY),
            pl.BlockSpec(memory_space=pltpu.SMEM),
            pl.BlockSpec(memory_space=pltpu.SMEM),
        ],
        out_specs=(pl.BlockSpec(memory_space=pl.ANY), pl.BlockSpec(memory_space=pltpu.SMEM)),
        scratch_shapes=[
            pltpu.VMEM((nb, planes + 4, gy, gz), f32),
            pltpu.VMEM((planes, gy, gz), f32),
            pltpu.VMEM((planes + 4, gy, gz), f32),
            pltpu.VMEM((2, nb, gy, gz), f32),
            pltpu.VMEM((2, nb, gy, gz), f32),
            pltpu.VMEM((npairs, planes + 4, gy + 2 * PAD, gz), f32),
            pltpu.VMEM((npairs, planes + 4, gy + 2 * PAD, gz), f32),
            pltpu.VMEM((npairs, planes + 2, gy + 2 * PAD, gz), f32),
            pltpu.VMEM((nb, planes, gy, gz), f32),
            pltpu.VMEM((slots, 8, gz), f32),
            dma((2,)),
            dma((planes,)),
            dma((2, 5)),
            dma((2, 5)),
            dma((2, 2)),
            dma((2, 2)),
            dma((slots,)),
            dma((slots,)),
        ],
        compiler_params=pltpu.CompilerParams(
            collective_id=0, has_side_effects=True, vmem_limit_bytes=63 * 1024 * 1024
        ),
    )(orbitals, screen, band_ids, occupations)
    return exchange, energy


def solution(mesh):
    in_specs = (P("grp", "band", None, None), P("grp"), P("grp"), P("band", None, None))
    out_specs = (P("grp", "band", None, None), P("grp"))
    return jax.shard_map(body, mesh=mesh, in_specs=in_specs, out_specs=out_specs, check_vma=False)
```

```python
import functools

import jax
import jax.numpy as jnp
from jax import lax
from jax.experimental import pallas as pl
from jax.experimental.pallas import tpu as pltpu
from jax.sharding import PartitionSpec as P

LO, HI = 0, 1
PAD = 8


def kernel(
    dims, cells,
    psi_hbm, screen_hbm, ids_ref, occs_ref, exch_hbm, energy_ref,
    psi, scr, c, usend, urecv, f1, f2, f3, ex, eslots,
    local_sem, out_sem, send_sem, recv_sem, fsend_sem, frecv_sem, esend_sem, erecv_sem,
):
    ngrp, n, nb, planes, gy, gz = dims
    pairs = [(i, j) for i in range(nb) for j in range(i, nb)]
    me = lax.axis_index("band")
    grp = lax.axis_index("grp")
    has = (me > 0, me < n - 1)
    near = (me - 1, me + 1)

    load_psi = pltpu.make_async_copy(psi_hbm, psi.at[:, pl.ds(2, planes)], local_sem.at[0])
    load_scr = pltpu.make_async_copy(screen_hbm, scr, local_sem.at[1])
    load_scr.start()
    load_psi.start()

    barrier = pltpu.get_barrier_semaphore()
    others = 0
    if ngrp == 2:
        pl.semaphore_signal(barrier, inc=1, device_id={"grp": 1 - grp})
        others += 1
    def greet(k, carry):
        pl.semaphore_signal(barrier, inc=1, device_id={"band": lax.rem(me + k, n)})
        return carry

    lax.fori_loop(1, n, greet, 0)
    others += n - 1

    rows = gy // 2 if ngrp == 2 else gy
    mine = pl.ds(pl.multiple_of(grp * rows, 8), rows) if ngrp == 2 else pl.ds(0, gy)
    theirs = pl.ds(pl.multiple_of((1 - grp) * rows, 8), rows) if ngrp == 2 else pl.ds(0, gy)

    def halo(side, depth):
        return 2 - depth if side == LO else planes + 1 + depth

    def own(side, depth):
        return planes - depth if side == LO else depth - 1

    def copy(side, number):
        depth = number // 2 + 1
        if number == 4:
            src, dst = usend.at[side], urecv.at[side]
        elif number % 2 == 0:
            src = psi_hbm.at[:, pl.ds(own(side, depth), 1)]
            dst = psi.at[:, pl.ds(halo(side, depth), 1)]
        else:
            src = c.at[own(side, depth) + 2, mine]
            dst = c.at[halo(side, depth), mine]
        return pltpu.make_async_remote_copy(
            src_ref=src, dst_ref=dst,
            send_sem=send_sem.at[side, number], recv_sem=recv_sem.at[side, number],
            device_id={"band": near[1 - side]},
        )

    def send(number):
        for side in (LO, HI):
            @pl.when(has[1 - side])
            def _():
                copy(side, number).start()

    def arrived(number):
        for side in (LO, HI):
            @pl.when(has[side])
            def _():
                copy(side, number).wait_recv()

    def forward(side, depth, rows_at):
        where = c.at[halo(side, depth), rows_at]
        return pltpu.make_async_remote_copy(
            src_ref=where, dst_ref=where,
            send_sem=fsend_sem.at[side, depth - 1], recv_sem=frecv_sem.at[side, depth - 1],
            device_id={"grp": 1 - grp},
        )

    def screen_arrived(depth):
        arrived(2 * depth - 1)
        if ngrp == 2:
            for side in (LO, HI):
                @pl.when(has[side])
                def _():
                    forward(side, depth, mine).start()
            for side in (LO, HI):
                @pl.when(has[side])
                def _():
                    forward(side, depth, theirs).wait_recv()

    load_scr.wait()
    for p in range(planes):
        c[p + 2] = 0.8 / (6.0 + scr[p])
    load_psi.wait()
    for side in (LO, HI):
        p = own(side, 3) + 2
        root = jnp.sqrt(c[p])
        for b in range(nb):
            usend[side, b] = root * psi[b, p]

    for side in (LO, HI):
        @pl.when(jnp.logical_not(has[side]))
        def _():
            at = 0 if side == LO else planes + 2
            for d in range(2):
                c[at + d] = jnp.zeros((gy, gz), jnp.float32)
                for b in range(nb):
                    psi[b, at + d] = jnp.zeros((gy, gz), jnp.float32)
            for b in range(nb):
                urecv[side, b] = jnp.zeros((gy, gz), jnp.float32)

    occ = []
    for s in range(nb):
        total = jnp.float32(0.0)
        for b in range(nb):
            total = total + jnp.where(ids_ref[s] == b, occs_ref[b], jnp.float32(0.0))
        occ.append(total)

    zeros = jnp.zeros((PAD, gz), jnp.float32)
    for buf in (f1, f2, f3):
        count = buf.shape[1]

        def clear(at, carry, buf=buf, count=count):
            for k in range(len(pairs)):
                buf[k, at, pl.ds(0, PAD)] = zeros
                buf[k, at, pl.ds(PAD + gy, PAD)] = zeros
            return carry

        lax.fori_loop(0, count, clear, 0)

    pl.semaphore_wait(barrier, others)
    for number in (1, 0, 3, 2, 4):
        send(number)

    lanes = lax.broadcasted_iota(jnp.int32, (gy, gz), 1)
    first, last = lanes == 0, lanes == gz - 1

    def lateral(buf, k, at):
        mid = buf[k, at, pl.ds(PAD, gy)]
        total = buf[k, at, pl.ds(PAD - 1, gy)] + buf[k, at, pl.ds(PAD + 1, gy)]
        total = total + jnp.where(first, 0.0, pltpu.roll(mid, 1, 1))
        total = total + jnp.where(last, 0.0, pltpu.roll(mid, gz - 1, 1))
        return mid, total

    def plane_pair(lo, hi):
        def each(body):
            def outer(t, carry):
                body(lo + t * (hi - lo), t)
                return carry

            lax.fori_loop(0, 2, outer, 0)

        return each

    def pairwise(body):
        for k, (i, j) in enumerate(pairs):
            body(k, i, j)

    def start_sweep(lo, hi):
        def plane(p, t):
            def one(k, i, j):
                f1[k, p, pl.ds(PAD, gy)] = c[p] * (psi[i, p] * psi[j, p])

            pairwise(one)

        plane_pair(lo, hi)(plane)

    def second(lo, hi, outer=False):
        def plane(p, t):
            def one(k, i, j):
                mid, total = lateral(f1, k, p)
                if outer:
                    total = total + f1[k, p + 1 - 2 * t, pl.ds(PAD, gy)]
                else:
                    total = total + f1[k, p - 1, pl.ds(PAD, gy)] + f1[k, p + 1, pl.ds(PAD, gy)]
                f2[k, p, pl.ds(PAD, gy)] = 1.2 * mid + c[p] * total

            pairwise(one)

        plane_pair(lo, hi)(plane)

    def third(lo, hi):
        def plane(p, t):
            def one(k, i, j):
                mid, total = lateral(f2, k, p)
                total = total + f2[k, p - 1, pl.ds(PAD, gy)] + f2[k, p + 1, pl.ds(PAD, gy)]
                total = total + psi[i, p] * psi[j, p]
                f3[k, p - 1, pl.ds(PAD, gy)] = 0.2 * mid + c[p] * total

            pairwise(one)

        plane_pair(lo, hi)(plane)

    def fourth(lo, hi):
        def plane(p, t):
            done = set()
            for k, (i, j) in enumerate(pairs):
                mid, total = lateral(f3, k, p - 1)
                total = total + f3[k, p - 2, pl.ds(PAD, gy)] + f3[k, p, pl.ds(PAD, gy)]
                total = total + psi[i, p] * psi[j, p]
                phi = 0.2 * mid + c[p] * total
                for a, b in {(i, j), (j, i)}:
                    term = (occ[b] * psi[b, p]) * phi
                    ex[a, p - 2] = ex[a, p - 2] - term if a in done else -term
                    done.add(a)

        plane_pair(lo, hi)(plane)

    m = planes - 1 + 2
    start_sweep(2, m)
    start_sweep(3, m - 1)
    second(3, m - 1)
    arrived(0)
    screen_arrived(1)
    start_sweep(1, m + 1)
    second(2, m)
    third(3, m - 1)
    arrived(2)
    screen_arrived(2)
    start_sweep(0, m + 2)
    second(1, m + 1)
    third(2, m)

    def energy_plane(p, acc):
        inverse = 1.25 * (6.0 + scr[p - 2])
        for k, (i, j) in enumerate(pairs):
            a, b, d = (buf[k, at, pl.ds(PAD, gy)] for buf, at in ((f1, p), (f2, p), (f3, p - 1)))
            weight = (1.0 if i == j else 2.0) * occ[i] * occ[j]
            value = psi[i, p] * psi[j, p] * b + (b - a) * (d - a) * inverse
            acc = acc + weight * jnp.sum(value.reshape(gy // 8, 8, gz), axis=0)
        return acc

    local = lax.fori_loop(2, planes + 2, energy_plane, jnp.zeros((8, gz), jnp.float32))

    def ecopy(slot, k):
        return pltpu.make_async_remote_copy(
            src_ref=eslots.at[me, pl.ds(0, 1)], dst_ref=eslots.at[slot, pl.ds(0, 1)],
            send_sem=esend_sem.at[k], recv_sem=erecv_sem.at[slot],
            device_id={"band": lax.rem(me + k, n)},
        )

    def each_peer(act):
        def step(k, carry):
            act(k)
            return carry

        lax.fori_loop(1, n, step, 0)

    eslots[me, pl.ds(0, 1)] = jnp.sum(local, axis=0, keepdims=True)
    each_peer(lambda k: ecopy(me, k).start())

    second(0, m + 2, outer=True)
    third(1, m + 1)
    fourth(3, m - 1)

    def out_copy(p, slot):
        return pltpu.make_async_copy(
            ex.at[:, pl.ds(p, 1)], exch_hbm.at[:, pl.ds(p, 1)], out_sem.at[slot]
        )

    for p in range(1, planes - 1):
        out_copy(p, p).start()
    fourth(2, m)

    arrived(4)
    for side in (LO, HI):
        p = 2 if side == LO else m
        step = -1 if side == LO else 1
        factor = c[p] * c[p + step] * c[p + 2 * step]
        total = sum((occ[b] * psi[b, p]) * urecv[side, b] for b in range(nb))
        total = total * factor
        for b in range(nb):
            ex[b, p - 2] = ex[b, p - 2] - total * urecv[side, b]
    for p in (0, planes - 1):
        out_copy(p, p).start()

    for number in range(5):
        for side in (LO, HI):
            @pl.when(has[1 - side])
            def _():
                copy(side, number).wait_send()
    if ngrp == 2:
        for depth in (1, 2):
            for side in (LO, HI):
                @pl.when(has[side])
                def _():
                    forward(side, depth, mine).wait_send()
    each_peer(lambda k: ecopy(lax.rem(me + k, n), k).wait_recv())
    energy_ref[0] = (-0.5 / cells) * jnp.sum(eslots[:, pl.ds(0, 1)])
    each_peer(lambda k: ecopy(me, k).wait_send())
    for p in range(planes):
        out_copy(p, p).wait()


def body(orbitals, band_ids, occupations, screen):
    nb, planes, gy, gz = orbitals.shape
    ngrp, n = lax.axis_size("grp"), lax.axis_size("band")
    npairs = nb * (nb + 1) // 2
    slots = n
    f32 = jnp.float32
    dma = pltpu.SemaphoreType.DMA
    exchange, energy = pl.pallas_call(
        functools.partial(kernel, (ngrp, n, nb, planes, gy, gz), float(planes * n * gy * gz)),
        out_shape=(
            jax.ShapeDtypeStruct((nb, planes, gy, gz), f32),
            jax.ShapeDtypeStruct((1,), f32),
        ),
        in_specs=[
            pl.BlockSpec(memory_space=pl.ANY),
            pl.BlockSpec(memory_space=pl.ANY),
            pl.BlockSpec(memory_space=pltpu.SMEM),
            pl.BlockSpec(memory_space=pltpu.SMEM),
        ],
        out_specs=(pl.BlockSpec(memory_space=pl.ANY), pl.BlockSpec(memory_space=pltpu.SMEM)),
        scratch_shapes=[
            pltpu.VMEM((nb, planes + 4, gy, gz), f32),
            pltpu.VMEM((planes, gy, gz), f32),
            pltpu.VMEM((planes + 4, gy, gz), f32),
            pltpu.VMEM((2, nb, gy, gz), f32),
            pltpu.VMEM((2, nb, gy, gz), f32),
            pltpu.VMEM((npairs, planes + 4, gy + 2 * PAD, gz), f32),
            pltpu.VMEM((npairs, planes + 4, gy + 2 * PAD, gz), f32),
            pltpu.VMEM((npairs, planes + 2, gy + 2 * PAD, gz), f32),
            pltpu.VMEM((nb, planes, gy, gz), f32),
            pltpu.VMEM((slots, 8, gz), f32),
            dma((2,)),
            dma((planes,)),
            dma((2, 5)),
            dma((2, 5)),
            dma((2, 2)),
            dma((2, 2)),
            dma((slots,)),
            dma((slots,)),
        ],
        compiler_params=pltpu.CompilerParams(
            collective_id=0, has_side_effects=True, vmem_limit_bytes=63 * 1024 * 1024
        ),
    )(orbitals, screen, band_ids, occupations)
    return exchange, energy


def solution(mesh):
    in_specs = (P("grp", "band", None, None), P("grp"), P("grp"), P("band", None, None))
    out_specs = (P("grp", "band", None, None), P("grp"))
    return jax.shard_map(body, mesh=mesh, in_specs=in_specs, out_specs=out_specs, check_vma=False)
```

```python
import functools

import jax
import jax.numpy as jnp
from jax import lax
from jax.experimental import pallas as pl
from jax.experimental.pallas import tpu as pltpu
from jax.sharding import PartitionSpec as P

LO, HI = 0, 1
PAD = 8


def kernel(
    dims, cells,
    psi_hbm, screen_hbm, ids_ref, occs_ref, exch_hbm, energy_ref,
    psi, scr, c, usend, urecv, f1, f2, f3, ex, eslots,
    local_sem, out_sem, send_sem, recv_sem, fsend_sem, frecv_sem, esend_sem, erecv_sem,
):
    ngrp, n, nb, planes, gy, gz = dims
    pairs = [(i, j) for i in range(nb) for j in range(i, nb)]
    me = lax.axis_index("band")
    grp = lax.axis_index("grp")
    has = (me > 0, me < n - 1)
    near = (me - 1, me + 1)

    load_psi = pltpu.make_async_copy(psi_hbm, psi.at[:, pl.ds(2, planes)], local_sem.at[0])
    load_scr = pltpu.make_async_copy(screen_hbm, scr, local_sem.at[1])
    load_scr.start()
    load_psi.start()

    barrier = pltpu.get_barrier_semaphore()
    others = 0
    if ngrp < 0:
        pl.semaphore_signal(barrier, inc=1, device_id={"grp": 1 - grp})
        others += 1
    def greet(k, carry):
        pl.semaphore_signal(barrier, inc=1, device_id={"band": lax.rem(me + k, n)})
        return carry

    lax.fori_loop(1, n, greet, 0)
    others += n - 1

    rows = gy // 2 if ngrp < 0 else gy
    mine = pl.ds(pl.multiple_of(grp * rows, 8), rows) if ngrp < 0 else pl.ds(0, gy)
    theirs = pl.ds(pl.multiple_of((1 - grp) * rows, 8), rows) if ngrp < 0 else pl.ds(0, gy)

    def halo(side, depth):
        return 2 - depth if side == LO else planes + 1 + depth

    def own(side, depth):
        return planes - depth if side == LO else depth - 1

    def copy(side, number):
        depth = number // 2 + 1
        if number == 4:
            src, dst = usend.at[side], urecv.at[side]
        elif number % 2 == 0:
            src = psi_hbm.at[:, pl.ds(own(side, depth), 1)]
            dst = psi.at[:, pl.ds(halo(side, depth), 1)]
        else:
            src = c.at[own(side, depth) + 2, mine]
            dst = c.at[halo(side, depth), mine]
        return pltpu.make_async_remote_copy(
            src_ref=src, dst_ref=dst,
            send_sem=send_sem.at[side, number], recv_sem=recv_sem.at[side, number],
            device_id={"band": near[1 - side]},
        )

    def send(number):
        for side in (LO, HI):
            @pl.when(has[1 - side])
            def _():
                copy(side, number).start()

    def sent(number):
        for side in (LO, HI):
            @pl.when(has[1 - side])
            def _():
                copy(side, number).wait_send()

    def arrived(number):
        for side in (LO, HI):
            @pl.when(has[side])
            def _():
                copy(side, number).wait_recv()

    def forward(side, depth, rows_at):
        where = c.at[halo(side, depth), rows_at]
        return pltpu.make_async_remote_copy(
            src_ref=where, dst_ref=where,
            send_sem=fsend_sem.at[side, depth - 1], recv_sem=frecv_sem.at[side, depth - 1],
            device_id={"grp": 1 - grp},
        )

    def screen_arrived(depth):
        arrived(2 * depth - 1)
        if ngrp < 0:
            for side in (LO, HI):
                @pl.when(has[side])
                def _():
                    forward(side, depth, mine).start()
            for side in (LO, HI):
                @pl.when(has[side])
                def _():
                    forward(side, depth, theirs).wait_recv()

    load_scr.wait()
    for p in range(planes):
        c[p + 2] = 0.8 / (6.0 + scr[p])
    load_psi.wait()
    for side in (LO, HI):
        p = own(side, 3) + 2
        root = jnp.sqrt(c[p])
        for b in range(nb):
            usend[side, b] = root * psi[b, p]

    for side in (LO, HI):
        @pl.when(jnp.logical_not(has[side]))
        def _():
            at = 0 if side == LO else planes + 2
            for d in range(2):
                c[at + d] = jnp.zeros((gy, gz), jnp.float32)
                for b in range(nb):
                    psi[b, at + d] = jnp.zeros((gy, gz), jnp.float32)
            for b in range(nb):
                urecv[side, b] = jnp.zeros((gy, gz), jnp.float32)

    occ = []
    for s in range(nb):
        total = jnp.float32(0.0)
        for b in range(nb):
            total = total + jnp.where(ids_ref[s] == b, occs_ref[b], jnp.float32(0.0))
        occ.append(total)

    zeros = jnp.zeros((PAD, gz), jnp.float32)
    for buf in (f1, f2, f3):
        count = buf.shape[1]

        def clear(at, carry, buf=buf, count=count):
            for k in range(len(pairs)):
                buf[k, at, pl.ds(0, PAD)] = zeros
                buf[k, at, pl.ds(PAD + gy, PAD)] = zeros
            return carry

        lax.fori_loop(0, count, clear, 0)

    pl.semaphore_wait(barrier, others)
    for number in (1, 0, 3, 2):
        send(number)

    lanes = lax.broadcasted_iota(jnp.int32, (gy, gz), 1)
    first, last = lanes == 0, lanes == gz - 1

    def lateral(buf, k, at):
        mid = buf[k, at, pl.ds(PAD, gy)]
        total = buf[k, at, pl.ds(PAD - 1, gy)] + buf[k, at, pl.ds(PAD + 1, gy)]
        total = total + jnp.where(first, 0.0, pltpu.roll(mid, 1, 1))
        total = total + jnp.where(last, 0.0, pltpu.roll(mid, gz - 1, 1))
        return mid, total

    def plane_pair(lo, hi):
        def each(body):
            def outer(t, carry):
                body(lo + t * (hi - lo), t)
                return carry

            lax.fori_loop(0, 2, outer, 0)

        return each

    def pairwise(body):
        for k, (i, j) in enumerate(pairs):
            body(k, i, j)

    def start_sweep(lo, hi):
        def plane(p, t):
            def one(k, i, j):
                f1[k, p, pl.ds(PAD, gy)] = c[p] * (psi[i, p] * psi[j, p])

            pairwise(one)

        plane_pair(lo, hi)(plane)

    def second(lo, hi, outer=False):
        def plane(p, t):
            def one(k, i, j):
                mid, total = lateral(f1, k, p)
                if outer:
                    total = total + f1[k, p + 1 - 2 * t, pl.ds(PAD, gy)]
                else:
                    total = total + f1[k, p - 1, pl.ds(PAD, gy)] + f1[k, p + 1, pl.ds(PAD, gy)]
                f2[k, p, pl.ds(PAD, gy)] = 1.2 * mid + c[p] * total

            pairwise(one)

        plane_pair(lo, hi)(plane)

    def third(lo, hi):
        def plane(p, t):
            def one(k, i, j):
                mid, total = lateral(f2, k, p)
                total = total + f2[k, p - 1, pl.ds(PAD, gy)] + f2[k, p + 1, pl.ds(PAD, gy)]
                total = total + psi[i, p] * psi[j, p]
                f3[k, p - 1, pl.ds(PAD, gy)] = 0.2 * mid + c[p] * total

            pairwise(one)

        plane_pair(lo, hi)(plane)

    def fourth(lo, hi):
        def plane(p, t):
            done = set()
            for k, (i, j) in enumerate(pairs):
                mid, total = lateral(f3, k, p - 1)
                total = total + f3[k, p - 2, pl.ds(PAD, gy)] + f3[k, p, pl.ds(PAD, gy)]
                total = total + psi[i, p] * psi[j, p]
                phi = 0.2 * mid + c[p] * total
                for a, b in {(i, j), (j, i)}:
                    term = (occ[b] * psi[b, p]) * phi
                    ex[a, p - 2] = ex[a, p - 2] - term if a in done else -term
                    done.add(a)

        plane_pair(lo, hi)(plane)

    m = planes - 1 + 2
    start_sweep(2, m)
    start_sweep(3, m - 1)
    second(3, m - 1)
    arrived(0)
    screen_arrived(1)
    start_sweep(1, m + 1)
    second(2, m)
    third(3, m - 1)
    sent(2)
    send(4)
    arrived(2)
    screen_arrived(2)
    start_sweep(0, m + 2)
    second(1, m + 1)
    third(2, m)

    def energy_plane(p, acc):
        inverse = 1.25 * (6.0 + scr[p - 2])
        for k, (i, j) in enumerate(pairs):
            a, b, d = (buf[k, at, pl.ds(PAD, gy)] for buf, at in ((f1, p), (f2, p), (f3, p - 1)))
            weight = (1.0 if i == j else 2.0) * occ[i] * occ[j]
            value = psi[i, p] * psi[j, p] * b + (b - a) * (d - a) * inverse
            acc = acc + weight * jnp.sum(value.reshape(gy // 8, 8, gz), axis=0)
        return acc

    local = lax.fori_loop(2, planes + 2, energy_plane, jnp.zeros((8, gz), jnp.float32))

    def ecopy(slot, k):
        return pltpu.make_async_remote_copy(
            src_ref=eslots.at[me, pl.ds(0, 1)], dst_ref=eslots.at[slot, pl.ds(0, 1)],
            send_sem=esend_sem.at[k], recv_sem=erecv_sem.at[slot],
            device_id={"band": lax.rem(me + k, n)},
        )

    def each_peer(act):
        def step(k, carry):
            act(k)
            return carry

        lax.fori_loop(1, n, step, 0)

    eslots[me, pl.ds(0, 1)] = jnp.sum(local, axis=0, keepdims=True)
    each_peer(lambda k: ecopy(me, k).start())

    second(0, m + 2, outer=True)
    third(1, m + 1)
    fourth(3, m - 1)

    def out_copy(p, slot):
        return pltpu.make_async_copy(
            ex.at[:, pl.ds(p, 1)], exch_hbm.at[:, pl.ds(p, 1)], out_sem.at[slot]
        )

    for p in range(1, planes - 1):
        out_copy(p, p).start()
    fourth(2, m)

    arrived(4)
    for side in (LO, HI):
        p = 2 if side == LO else m
        step = -1 if side == LO else 1
        factor = c[p] * c[p + step] * c[p + 2 * step]
        total = sum((occ[b] * psi[b, p]) * urecv[side, b] for b in range(nb))
        total = total * factor
        for b in range(nb):
            ex[b, p - 2] = ex[b, p - 2] - total * urecv[side, b]
    for p in (0, planes - 1):
        out_copy(p, p).start()

    for number in (0, 1, 3, 4):
        sent(number)
    if ngrp < 0:
        for depth in (1, 2):
            for side in (LO, HI):
                @pl.when(has[side])
                def _():
                    forward(side, depth, mine).wait_send()
    each_peer(lambda k: ecopy(lax.rem(me + k, n), k).wait_recv())
    energy_ref[0] = (-0.5 / cells) * jnp.sum(eslots[:, pl.ds(0, 1)])
    each_peer(lambda k: ecopy(me, k).wait_send())
    for p in range(planes):
        out_copy(p, p).wait()


def body(orbitals, band_ids, occupations, screen):
    nb, planes, gy, gz = orbitals.shape
    ngrp, n = lax.axis_size("grp"), lax.axis_size("band")
    npairs = nb * (nb + 1) // 2
    slots = n
    f32 = jnp.float32
    dma = pltpu.SemaphoreType.DMA
    exchange, energy = pl.pallas_call(
        functools.partial(kernel, (ngrp, n, nb, planes, gy, gz), float(planes * n * gy * gz)),
        out_shape=(
            jax.ShapeDtypeStruct((nb, planes, gy, gz), f32),
            jax.ShapeDtypeStruct((1,), f32),
        ),
        in_specs=[
            pl.BlockSpec(memory_space=pl.ANY),
            pl.BlockSpec(memory_space=pl.ANY),
            pl.BlockSpec(memory_space=pltpu.SMEM),
            pl.BlockSpec(memory_space=pltpu.SMEM),
        ],
        out_specs=(pl.BlockSpec(memory_space=pl.ANY), pl.BlockSpec(memory_space=pltpu.SMEM)),
        scratch_shapes=[
            pltpu.VMEM((nb, planes + 4, gy, gz), f32),
            pltpu.VMEM((planes, gy, gz), f32),
            pltpu.VMEM((planes + 4, gy, gz), f32),
            pltpu.VMEM((2, nb, gy, gz), f32),
            pltpu.VMEM((2, nb, gy, gz), f32),
            pltpu.VMEM((npairs, planes + 4, gy + 2 * PAD, gz), f32),
            pltpu.VMEM((npairs, planes + 4, gy + 2 * PAD, gz), f32),
            pltpu.VMEM((npairs, planes + 2, gy + 2 * PAD, gz), f32),
            pltpu.VMEM((nb, planes, gy, gz), f32),
            pltpu.VMEM((slots, 8, gz), f32),
            dma((2,)),
            dma((planes,)),
            dma((2, 5)),
            dma((2, 5)),
            dma((2, 2)),
            dma((2, 2)),
            dma((slots,)),
            dma((slots,)),
        ],
        compiler_params=pltpu.CompilerParams(
            collective_id=0, has_side_effects=True, vmem_limit_bytes=63 * 1024 * 1024
        ),
    )(orbitals, screen, band_ids, occupations)
    return exchange, energy


def solution(mesh):
    in_specs = (P("grp", "band", None, None), P("grp"), P("grp"), P("band", None, None))
    out_specs = (P("grp", "band", None, None), P("grp"))
    return jax.shard_map(body, mesh=mesh, in_specs=in_specs, out_specs=out_specs, check_vma=False)
```

```python
import functools

import jax
import jax.numpy as jnp
from jax import lax
from jax.experimental import pallas as pl
from jax.experimental.pallas import tpu as pltpu
from jax.sharding import PartitionSpec as P

LO, HI = 0, 1
PAD = 8


def kernel(
    dims, cells,
    psi_hbm, screen_hbm, ids_ref, occs_ref, exch_hbm, energy_ref,
    psi, scr, c, usend, urecv, f1, f2, f3, ex, eslots,
    local_sem, out_sem, send_sem, recv_sem, fsend_sem, frecv_sem, esend_sem, erecv_sem,
):
    ngrp, n, nb, planes, gy, gz = dims
    pairs = [(i, j) for i in range(nb) for j in range(i, nb)]
    me = lax.axis_index("band")
    grp = lax.axis_index("grp")
    has = (me > 0, me < n - 1)
    near = (me - 1, me + 1)

    load_psi = pltpu.make_async_copy(psi_hbm, psi.at[:, pl.ds(2, planes)], local_sem.at[0])
    load_scr = pltpu.make_async_copy(screen_hbm, scr, local_sem.at[1])
    load_scr.start()
    load_psi.start()

    barrier = pltpu.get_barrier_semaphore()
    others = 0
    if ngrp == 2:
        pl.semaphore_signal(barrier, inc=1, device_id={"grp": 1 - grp})
        others += 1
    def greet(k, carry):
        pl.semaphore_signal(barrier, inc=1, device_id={"band": lax.rem(me + k, n)})
        return carry

    lax.fori_loop(1, n, greet, 0)
    others += n - 1

    rows = gy // 2 if ngrp == 2 else gy
    mine = pl.ds(pl.multiple_of(grp * rows, 8), rows) if ngrp == 2 else pl.ds(0, gy)
    theirs = pl.ds(pl.multiple_of((1 - grp) * rows, 8), rows) if ngrp == 2 else pl.ds(0, gy)

    def halo(side, depth):
        return 2 - depth if side == LO else planes + 1 + depth

    def own(side, depth):
        return planes - depth if side == LO else depth - 1

    def copy(side, number):
        depth = number // 2 + 1
        if number == 4:
            src, dst = usend.at[side], urecv.at[side]
        elif number % 2 == 0:
            src = psi_hbm.at[:, pl.ds(own(side, depth), 1)]
            dst = psi.at[:, pl.ds(halo(side, depth), 1)]
        else:
            part = mine
            src = c.at[own(side, depth) + 2, part]
            dst = c.at[halo(side, depth), part]
        return pltpu.make_async_remote_copy(
            src_ref=src, dst_ref=dst,
            send_sem=send_sem.at[side, number], recv_sem=recv_sem.at[side, number],
            device_id={"band": near[1 - side]},
        )

    def send(number):
        for side in (LO, HI):
            @pl.when(has[1 - side])
            def _():
                copy(side, number).start()

    def sent(number):
        for side in (LO, HI):
            @pl.when(has[1 - side])
            def _():
                copy(side, number).wait_send()

    def arrived(number):
        for side in (LO, HI):
            @pl.when(has[side])
            def _():
                copy(side, number).wait_recv()

    def forward(side, depth, rows_at):
        where = c.at[halo(side, depth), rows_at]
        return pltpu.make_async_remote_copy(
            src_ref=where, dst_ref=where,
            send_sem=fsend_sem.at[side, depth - 1], recv_sem=frecv_sem.at[side, depth - 1],
            device_id={"grp": 1 - grp},
        )

    def halves(act):
        if ngrp == 2:
            for side in (LO, HI):
                @pl.when(has[side])
                def _():
                    act(side)

    load_scr.wait()
    for p in range(planes):
        c[p + 2] = 0.8 / (6.0 + scr[p])
    load_psi.wait()
    for side in (LO, HI):
        p = own(side, 3) + 2
        root = jnp.sqrt(c[p])
        for b in range(nb):
            usend[side, b] = root * psi[b, p]

    for side in (LO, HI):
        @pl.when(jnp.logical_not(has[side]))
        def _():
            at = 0 if side == LO else planes + 2
            for d in range(2):
                c[at + d] = jnp.zeros((gy, gz), jnp.float32)
                for b in range(nb):
                    psi[b, at + d] = jnp.zeros((gy, gz), jnp.float32)
            for b in range(nb):
                urecv[side, b] = jnp.zeros((gy, gz), jnp.float32)

    occ = []
    for s in range(nb):
        total = jnp.float32(0.0)
        for b in range(nb):
            total = total + jnp.where(ids_ref[s] == b, occs_ref[b], jnp.float32(0.0))
        occ.append(total)

    zeros = jnp.zeros((PAD, gz), jnp.float32)
    for buf in (f1, f2, f3):
        count = buf.shape[1]

        def clear(at, carry, buf=buf, count=count):
            for k in range(len(pairs)):
                buf[k, at, pl.ds(0, PAD)] = zeros
                buf[k, at, pl.ds(PAD + gy, PAD)] = zeros
            return carry

        lax.fori_loop(0, count, clear, 0)

    pl.semaphore_wait(barrier, others)
    for number in (1, 3, 0):
        send(number)

    lanes = lax.broadcasted_iota(jnp.int32, (gy, gz), 1)
    first, last = lanes == 0, lanes == gz - 1

    def lateral(buf, k, at):
        mid = buf[k, at, pl.ds(PAD, gy)]
        total = buf[k, at, pl.ds(PAD - 1, gy)] + buf[k, at, pl.ds(PAD + 1, gy)]
        total = total + jnp.where(first, 0.0, pltpu.roll(mid, 1, 1))
        total = total + jnp.where(last, 0.0, pltpu.roll(mid, gz - 1, 1))
        return mid, total

    def plane_pair(lo, hi):
        def each(body):
            def outer(t, carry):
                body(lo + t * (hi - lo), t)
                return carry

            lax.fori_loop(0, 2, outer, 0)

        return each

    def pairwise(body):
        for k, (i, j) in enumerate(pairs):
            body(k, i, j)

    def start_sweep(lo, hi):
        def plane(p, t):
            def one(k, i, j):
                f1[k, p, pl.ds(PAD, gy)] = c[p] * (psi[i, p] * psi[j, p])

            pairwise(one)

        plane_pair(lo, hi)(plane)

    def second(lo, hi, outer=False):
        def plane(p, t):
            def one(k, i, j):
                mid, total = lateral(f1, k, p)
                if outer:
                    total = total + f1[k, p + 1 - 2 * t, pl.ds(PAD, gy)]
                else:
                    total = total + f1[k, p - 1, pl.ds(PAD, gy)] + f1[k, p + 1, pl.ds(PAD, gy)]
                f2[k, p, pl.ds(PAD, gy)] = 1.2 * mid + c[p] * total

            pairwise(one)

        plane_pair(lo, hi)(plane)

    def third(lo, hi):
        def plane(p, t):
            def one(k, i, j):
                mid, total = lateral(f2, k, p)
                total = total + f2[k, p - 1, pl.ds(PAD, gy)] + f2[k, p + 1, pl.ds(PAD, gy)]
                total = total + psi[i, p] * psi[j, p]
                f3[k, p - 1, pl.ds(PAD, gy)] = 0.2 * mid + c[p] * total

            pairwise(one)

        plane_pair(lo, hi)(plane)

    def fourth(lo, hi):
        def plane(p, t):
            done = set()
            for k, (i, j) in enumerate(pairs):
                mid, total = lateral(f3, k, p - 1)
                total = total + f3[k, p - 2, pl.ds(PAD, gy)] + f3[k, p, pl.ds(PAD, gy)]
                total = total + psi[i, p] * psi[j, p]
                phi = 0.2 * mid + c[p] * total
                for a, b in {(i, j), (j, i)}:
                    term = (occ[b] * psi[b, p]) * phi
                    ex[a, p - 2] = ex[a, p - 2] - term if a in done else -term
                    done.add(a)

        plane_pair(lo, hi)(plane)

    m = planes - 1 + 2
    start_sweep(2, m)
    start_sweep(3, m - 1)
    second(3, m - 1)
    for depth in (1, 2):
        arrived(2 * depth - 1)
        halves(lambda side: forward(side, depth, mine).start())
    send(2)
    arrived(0)
    halves(lambda side: forward(side, 1, theirs).wait_recv())
    start_sweep(1, m + 1)
    second(2, m)
    third(3, m - 1)
    sent(2)
    send(4)
    arrived(2)
    halves(lambda side: forward(side, 2, theirs).wait_recv())
    start_sweep(0, m + 2)
    second(1, m + 1)
    third(2, m)

    def energy_plane(p, acc):
        inverse = 1.25 * (6.0 + scr[p - 2])
        for k, (i, j) in enumerate(pairs):
            a, b, d = (buf[k, at, pl.ds(PAD, gy)] for buf, at in ((f1, p), (f2, p), (f3, p - 1)))
            weight = (1.0 if i == j else 2.0) * occ[i] * occ[j]
            value = psi[i, p] * psi[j, p] * b + (b - a) * (d - a) * inverse
            acc = acc + weight * jnp.sum(value.reshape(gy // 8, 8, gz), axis=0)
        return acc

    local = lax.fori_loop(2, planes + 2, energy_plane, jnp.zeros((8, gz), jnp.float32))

    def ecopy(slot, k):
        return pltpu.make_async_remote_copy(
            src_ref=eslots.at[me, pl.ds(0, 1)], dst_ref=eslots.at[slot, pl.ds(0, 1)],
            send_sem=esend_sem.at[k], recv_sem=erecv_sem.at[slot],
            device_id={"band": lax.rem(me + k, n)},
        )

    def each_peer(act):
        def step(k, carry):
            act(k)
            return carry

        lax.fori_loop(1, n, step, 0)

    eslots[me, pl.ds(0, 1)] = jnp.sum(local, axis=0, keepdims=True)
    each_peer(lambda k: ecopy(me, k).start())

    second(0, m + 2, outer=True)
    third(1, m + 1)
    fourth(3, m - 1)

    def out_copy(p, slot):
        return pltpu.make_async_copy(
            ex.at[:, pl.ds(p, 1)], exch_hbm.at[:, pl.ds(p, 1)], out_sem.at[slot]
        )

    for p in range(1, planes - 1):
        out_copy(p, p).start()
    fourth(2, m)

    arrived(4)
    for side in (LO, HI):
        p = 2 if side == LO else m
        step = -1 if side == LO else 1
        factor = c[p] * c[p + step] * c[p + 2 * step]
        total = sum((occ[b] * psi[b, p]) * urecv[side, b] for b in range(nb))
        total = total * factor
        for b in range(nb):
            ex[b, p - 2] = ex[b, p - 2] - total * urecv[side, b]
    for p in (0, planes - 1):
        out_copy(p, p).start()

    for number in (0, 1, 3, 4):
        sent(number)
    for depth in (1, 2):
        halves(lambda side: forward(side, depth, mine).wait_send())
    each_peer(lambda k: ecopy(lax.rem(me + k, n), k).wait_recv())
    energy_ref[0] = (-0.5 / cells) * jnp.sum(eslots[:, pl.ds(0, 1)])
    each_peer(lambda k: ecopy(me, k).wait_send())
    for p in range(planes):
        out_copy(p, p).wait()


def body(orbitals, band_ids, occupations, screen):
    nb, planes, gy, gz = orbitals.shape
    ngrp, n = lax.axis_size("grp"), lax.axis_size("band")
    npairs = nb * (nb + 1) // 2
    slots = n
    f32 = jnp.float32
    dma = pltpu.SemaphoreType.DMA
    exchange, energy = pl.pallas_call(
        functools.partial(kernel, (ngrp, n, nb, planes, gy, gz), float(planes * n * gy * gz)),
        out_shape=(
            jax.ShapeDtypeStruct((nb, planes, gy, gz), f32),
            jax.ShapeDtypeStruct((1,), f32),
        ),
        in_specs=[
            pl.BlockSpec(memory_space=pl.ANY),
            pl.BlockSpec(memory_space=pl.ANY),
            pl.BlockSpec(memory_space=pltpu.SMEM),
            pl.BlockSpec(memory_space=pltpu.SMEM),
        ],
        out_specs=(pl.BlockSpec(memory_space=pl.ANY), pl.BlockSpec(memory_space=pltpu.SMEM)),
        scratch_shapes=[
            pltpu.VMEM((nb, planes + 4, gy, gz), f32),
            pltpu.VMEM((planes, gy, gz), f32),
            pltpu.VMEM((planes + 4, gy, gz), f32),
            pltpu.VMEM((2, nb, gy, gz), f32),
            pltpu.VMEM((2, nb, gy, gz), f32),
            pltpu.VMEM((npairs, planes + 4, gy + 2 * PAD, gz), f32),
            pltpu.VMEM((npairs, planes + 4, gy + 2 * PAD, gz), f32),
            pltpu.VMEM((npairs, planes + 2, gy + 2 * PAD, gz), f32),
            pltpu.VMEM((nb, planes, gy, gz), f32),
            pltpu.VMEM((slots, 8, gz), f32),
            dma((2,)),
            dma((planes,)),
            dma((2, 5)),
            dma((2, 5)),
            dma((2, 2)),
            dma((2, 2)),
            dma((slots,)),
            dma((slots,)),
        ],
        compiler_params=pltpu.CompilerParams(
            collective_id=0, has_side_effects=True, vmem_limit_bytes=63 * 1024 * 1024
        ),
    )(orbitals, screen, band_ids, occupations)
    return exchange, energy


def solution(mesh):
    in_specs = (P("grp", "band", None, None), P("grp"), P("grp"), P("band", None, None))
    out_specs = (P("grp", "band", None, None), P("grp"))
    return jax.shard_map(body, mesh=mesh, in_specs=in_specs, out_specs=out_specs, check_vma=False)
```

```python
import functools

import jax
import jax.numpy as jnp
from jax import lax
from jax.experimental import pallas as pl
from jax.experimental.pallas import tpu as pltpu
from jax.sharding import PartitionSpec as P

LO, HI = 0, 1
PAD = 8


def kernel(
    dims, cells,
    psi_hbm, screen_hbm, ids_ref, occs_ref, exch_hbm, energy_ref,
    psi, scr, c, usend, urecv, f1, f2, f3, ex, eslots,
    local_sem, out_sem, send_sem, recv_sem, fsend_sem, frecv_sem, esend_sem, erecv_sem,
):
    ngrp, n, nb, planes, gy, gz = dims
    pairs = [(i, j) for i in range(nb) for j in range(i, nb)]
    me = lax.axis_index("band")
    grp = lax.axis_index("grp")
    has = (me > 0, me < n - 1)
    near = (me - 1, me + 1)

    load_psi = pltpu.make_async_copy(psi_hbm, psi.at[:, pl.ds(2, planes)], local_sem.at[0])
    load_scr = pltpu.make_async_copy(screen_hbm, scr, local_sem.at[1])
    load_scr.start()
    load_psi.start()

    barrier = pltpu.get_barrier_semaphore()
    others = 0
    if ngrp == 2:
        pl.semaphore_signal(barrier, inc=1, device_id={"grp": 1 - grp})
        others += 1
    def greet(k, carry):
        pl.semaphore_signal(barrier, inc=1, device_id={"band": lax.rem(me + k, n)})
        return carry

    lax.fori_loop(1, n, greet, 0)
    others += n - 1

    rows = gy // 2 if ngrp == 2 else gy
    mine = pl.ds(pl.multiple_of(grp * rows, 8), rows) if ngrp == 2 else pl.ds(0, gy)
    theirs = pl.ds(pl.multiple_of((1 - grp) * rows, 8), rows) if ngrp == 2 else pl.ds(0, gy)

    def halo(side, depth):
        return 2 - depth if side == LO else planes + 1 + depth

    def own(side, depth):
        return planes - depth if side == LO else depth - 1

    def copy(side, number):
        depth = number // 2 + 1
        if number >= 4:
            some = pl.ds(0, nb - 1) if number == 4 else pl.ds(nb - 1, 1)
            src, dst = usend.at[side, some], urecv.at[side, some]
        elif number % 2 == 0:
            src = psi_hbm.at[:, pl.ds(own(side, depth), 1)]
            dst = psi.at[:, pl.ds(halo(side, depth), 1)]
        else:
            part = mine
            src = c.at[own(side, depth) + 2, part]
            dst = c.at[halo(side, depth), part]
        return pltpu.make_async_remote_copy(
            src_ref=src, dst_ref=dst,
            send_sem=send_sem.at[side, number], recv_sem=recv_sem.at[side, number],
            device_id={"band": near[1 - side]},
        )

    def send(number):
        for side in (LO, HI):
            @pl.when(has[1 - side])
            def _():
                copy(side, number).start()

    def sent(number):
        for side in (LO, HI):
            @pl.when(has[1 - side])
            def _():
                copy(side, number).wait_send()

    def arrived(number):
        for side in (LO, HI):
            @pl.when(has[side])
            def _():
                copy(side, number).wait_recv()

    def forward(side, depth, rows_at):
        where = c.at[halo(side, depth), rows_at]
        return pltpu.make_async_remote_copy(
            src_ref=where, dst_ref=where,
            send_sem=fsend_sem.at[side, depth - 1], recv_sem=frecv_sem.at[side, depth - 1],
            device_id={"grp": 1 - grp},
        )

    def halves(act):
        if ngrp == 2:
            for side in (LO, HI):
                @pl.when(has[side])
                def _():
                    act(side)

    load_scr.wait()
    for p in range(planes):
        c[p + 2] = 0.8 / (6.0 + scr[p])
    load_psi.wait()
    for side in (LO, HI):
        p = own(side, 3) + 2
        root = jnp.sqrt(c[p])
        for b in range(nb):
            usend[side, b] = root * psi[b, p]

    for side in (LO, HI):
        @pl.when(jnp.logical_not(has[side]))
        def _():
            at = 0 if side == LO else planes + 2
            for d in range(2):
                c[at + d] = jnp.zeros((gy, gz), jnp.float32)
                for b in range(nb):
                    psi[b, at + d] = jnp.zeros((gy, gz), jnp.float32)
            for b in range(nb):
                urecv[side, b] = jnp.zeros((gy, gz), jnp.float32)

    occ = []
    for s in range(nb):
        total = jnp.float32(0.0)
        for b in range(nb):
            total = total + jnp.where(ids_ref[s] == b, occs_ref[b], jnp.float32(0.0))
        occ.append(total)

    zeros = jnp.zeros((PAD, gz), jnp.float32)
    for buf in (f1, f2, f3):
        count = buf.shape[1]

        def clear(at, carry, buf=buf, count=count):
            for k in range(len(pairs)):
                buf[k, at, pl.ds(0, PAD)] = zeros
                buf[k, at, pl.ds(PAD + gy, PAD)] = zeros
            return carry

        lax.fori_loop(0, count, clear, 0)

    pl.semaphore_wait(barrier, others)
    for number in (1, 3, 0):
        send(number)

    lanes = lax.broadcasted_iota(jnp.int32, (gy, gz), 1)
    first, last = lanes == 0, lanes == gz - 1

    def lateral(buf, k, at):
        mid = buf[k, at, pl.ds(PAD, gy)]
        total = buf[k, at, pl.ds(PAD - 1, gy)] + buf[k, at, pl.ds(PAD + 1, gy)]
        total = total + jnp.where(first, 0.0, pltpu.roll(mid, 1, 1))
        total = total + jnp.where(last, 0.0, pltpu.roll(mid, gz - 1, 1))
        return mid, total

    def plane_pair(lo, hi):
        def each(body):
            def outer(t, carry):
                body(lo + t * (hi - lo), t)
                return carry

            lax.fori_loop(0, 2, outer, 0)

        return each

    def pairwise(body):
        for k, (i, j) in enumerate(pairs):
            body(k, i, j)

    def start_sweep(lo, hi):
        def plane(p, t):
            def one(k, i, j):
                f1[k, p, pl.ds(PAD, gy)] = c[p] * (psi[i, p] * psi[j, p])

            pairwise(one)

        plane_pair(lo, hi)(plane)

    def second(lo, hi, outer=False):
        def plane(p, t):
            def one(k, i, j):
                mid, total = lateral(f1, k, p)
                if outer:
                    total = total + f1[k, p + 1 - 2 * t, pl.ds(PAD, gy)]
                else:
                    total = total + f1[k, p - 1, pl.ds(PAD, gy)] + f1[k, p + 1, pl.ds(PAD, gy)]
                f2[k, p, pl.ds(PAD, gy)] = 1.2 * mid + c[p] * total

            pairwise(one)

        plane_pair(lo, hi)(plane)

    def third(lo, hi):
        def plane(p, t):
            def one(k, i, j):
                mid, total = lateral(f2, k, p)
                total = total + f2[k, p - 1, pl.ds(PAD, gy)] + f2[k, p + 1, pl.ds(PAD, gy)]
                total = total + psi[i, p] * psi[j, p]
                f3[k, p - 1, pl.ds(PAD, gy)] = 0.2 * mid + c[p] * total

            pairwise(one)

        plane_pair(lo, hi)(plane)

    def fourth(lo, hi):
        def plane(p, t):
            done = set()
            for k, (i, j) in enumerate(pairs):
                mid, total = lateral(f3, k, p - 1)
                total = total + f3[k, p - 2, pl.ds(PAD, gy)] + f3[k, p, pl.ds(PAD, gy)]
                total = total + psi[i, p] * psi[j, p]
                phi = 0.2 * mid + c[p] * total
                for a, b in {(i, j), (j, i)}:
                    term = (occ[b] * psi[b, p]) * phi
                    ex[a, p - 2] = ex[a, p - 2] - term if a in done else -term
                    done.add(a)

        plane_pair(lo, hi)(plane)

    m = planes - 1 + 2
    start_sweep(2, m)
    start_sweep(3, m - 1)
    second(3, m - 1)
    for depth in (1, 2):
        arrived(2 * depth - 1)
        halves(lambda side: forward(side, depth, mine).start())
    send(2)
    send(5)
    arrived(0)
    halves(lambda side: forward(side, 1, theirs).wait_recv())
    start_sweep(1, m + 1)
    second(2, m)
    third(3, m - 1)
    sent(2)
    send(4)
    arrived(2)
    halves(lambda side: forward(side, 2, theirs).wait_recv())
    start_sweep(0, m + 2)
    second(1, m + 1)
    third(2, m)

    def energy_plane(p, acc):
        inverse = 1.25 * (6.0 + scr[p - 2])
        for k, (i, j) in enumerate(pairs):
            a, b, d = (buf[k, at, pl.ds(PAD, gy)] for buf, at in ((f1, p), (f2, p), (f3, p - 1)))
            weight = (1.0 if i == j else 2.0) * occ[i] * occ[j]
            value = psi[i, p] * psi[j, p] * b + (b - a) * (d - a) * inverse
            acc = acc + weight * jnp.sum(value.reshape(gy // 8, 8, gz), axis=0)
        return acc

    local = lax.fori_loop(2, planes + 2, energy_plane, jnp.zeros((8, gz), jnp.float32))

    def ecopy(slot, k):
        return pltpu.make_async_remote_copy(
            src_ref=eslots.at[me, pl.ds(0, 1)], dst_ref=eslots.at[slot, pl.ds(0, 1)],
            send_sem=esend_sem.at[k], recv_sem=erecv_sem.at[slot],
            device_id={"band": lax.rem(me + k, n)},
        )

    def each_peer(act):
        def step(k, carry):
            act(k)
            return carry

        lax.fori_loop(1, n, step, 0)

    eslots[me, pl.ds(0, 1)] = jnp.sum(local, axis=0, keepdims=True)
    each_peer(lambda k: ecopy(me, k).start())

    second(0, m + 2, outer=True)
    third(1, m + 1)
    fourth(3, m - 1)

    def out_copy(p, slot):
        return pltpu.make_async_copy(
            ex.at[:, pl.ds(p, 1)], exch_hbm.at[:, pl.ds(p, 1)], out_sem.at[slot]
        )

    for p in range(1, planes - 1):
        out_copy(p, p).start()
    fourth(2, m)

    arrived(4)
    arrived(5)
    for side in (LO, HI):
        p = 2 if side == LO else m
        step = -1 if side == LO else 1
        factor = c[p] * c[p + step] * c[p + 2 * step]
        total = sum((occ[b] * psi[b, p]) * urecv[side, b] for b in range(nb))
        total = total * factor
        for b in range(nb):
            ex[b, p - 2] = ex[b, p - 2] - total * urecv[side, b]
    for p in (0, planes - 1):
        out_copy(p, p).start()

    for number in (0, 1, 3, 4, 5):
        sent(number)
    for depth in (1, 2):
        halves(lambda side: forward(side, depth, mine).wait_send())
    each_peer(lambda k: ecopy(lax.rem(me + k, n), k).wait_recv())
    energy_ref[0] = (-0.5 / cells) * jnp.sum(eslots[:, pl.ds(0, 1)])
    each_peer(lambda k: ecopy(me, k).wait_send())
    for p in range(planes):
        out_copy(p, p).wait()


def body(orbitals, band_ids, occupations, screen):
    nb, planes, gy, gz = orbitals.shape
    ngrp, n = lax.axis_size("grp"), lax.axis_size("band")
    npairs = nb * (nb + 1) // 2
    slots = n
    f32 = jnp.float32
    dma = pltpu.SemaphoreType.DMA
    exchange, energy = pl.pallas_call(
        functools.partial(kernel, (ngrp, n, nb, planes, gy, gz), float(planes * n * gy * gz)),
        out_shape=(
            jax.ShapeDtypeStruct((nb, planes, gy, gz), f32),
            jax.ShapeDtypeStruct((1,), f32),
        ),
        in_specs=[
            pl.BlockSpec(memory_space=pl.ANY),
            pl.BlockSpec(memory_space=pl.ANY),
            pl.BlockSpec(memory_space=pltpu.SMEM),
            pl.BlockSpec(memory_space=pltpu.SMEM),
        ],
        out_specs=(pl.BlockSpec(memory_space=pl.ANY), pl.BlockSpec(memory_space=pltpu.SMEM)),
        scratch_shapes=[
            pltpu.VMEM((nb, planes + 4, gy, gz), f32),
            pltpu.VMEM((planes, gy, gz), f32),
            pltpu.VMEM((planes + 4, gy, gz), f32),
            pltpu.VMEM((2, nb, gy, gz), f32),
            pltpu.VMEM((2, nb, gy, gz), f32),
            pltpu.VMEM((npairs, planes + 4, gy + 2 * PAD, gz), f32),
            pltpu.VMEM((npairs, planes + 4, gy + 2 * PAD, gz), f32),
            pltpu.VMEM((npairs, planes + 2, gy + 2 * PAD, gz), f32),
            pltpu.VMEM((nb, planes, gy, gz), f32),
            pltpu.VMEM((slots, 8, gz), f32),
            dma((2,)),
            dma((planes,)),
            dma((2, 6)),
            dma((2, 6)),
            dma((2, 2)),
            dma((2, 2)),
            dma((slots,)),
            dma((slots,)),
        ],
        compiler_params=pltpu.CompilerParams(
            collective_id=0, has_side_effects=True, vmem_limit_bytes=63 * 1024 * 1024
        ),
    )(orbitals, screen, band_ids, occupations)
    return exchange, energy


def solution(mesh):
    in_specs = (P("grp", "band", None, None), P("grp"), P("grp"), P("band", None, None))
    out_specs = (P("grp", "band", None, None), P("grp"))
    return jax.shard_map(body, mesh=mesh, in_specs=in_specs, out_specs=out_specs, check_vma=False)
```
